512 devices in a mesh: row: 16 (over z_lo, y), col: 32 (over x, z_hi, core).
Axes of the slice: x: 4, y: 4, z: 16 (z_hi: 4, z_lo: 4; z = z_hi * 4 + z_lo), core: 2. Of those that a mesh axis runs over, the one named last changes fastest.
Arguments:
- hamiltonian: bfloat16 [2048, 65536], P('row', 'col'), may hold values from -0.125 to 0.125
- z_panel: bfloat16 [65536, 4096], P('row', 'col'), may hold values from -6 to 6
- z_slab: bfloat16 [2048, 4096], P('row', 'col'), may hold values from -0.125 to 0.125
- mask_h: int32 [32, 1024], P('row', 'col'), may hold values 0 or 1
- mask_panel: int32 [1024, 64], P('row', 'col'), may hold values 0 or 1
- mask_slab: int32 [32, 64], P('row', 'col'), may hold values 0 or 1
- section_blocks: int32 [2, 16], replicated, may hold values from 0 to 1023, as said below
Outputs:
- k_transposed: bfloat16 [4096, 4096], P('row', 'col')
The draws below stay inside these ranges and needn't reach their ends.
Inputs may be any that keep to these rules, and one draw needn't show every extreme that they name: `section_blocks`: each row holds 16 distinct block indices that all lie in one aligned group of 32 consecutive inner blocks; different rows lie in different groups.
All inputs are finite; a program needn't handle non-finite values. No bound on the sum of `mask_h` or of `mask_panel` or of `mask_slab` on one device may be relied on, other than what follows from the above.
Results may differ from the reference program's by a relative error of at most 0.018.
Values may be sent and summed in bfloat16 or wider, within the bound.
No kernel may reach another device: no remote copies, remote signals or barrier semaphores. Data moves between devices by JAX's collectives and lax.ppermute only.
A program may use at most 64 MiB of HBM per device.

```python
import jax
import jax.numpy as jnp
from jax import lax

BS = 64
RB = 2
SECTIONS = 2
NA = 32
PB = 16
IBH = 32
NJ = 64
IN = 1024
N_ROW = 16
N_COL = 32


def draw_section_blocks(key, part):
    key = jax.random.fold_in(key, 7)
    key_owner, key_turn, key_local = jax.random.split(key, 3)
    others = jax.random.permutation(key_owner, N_COL - 1)[:SECTIONS - 1].astype(jnp.int32)
    owners = jnp.concatenate([others, jnp.full((1,), N_COL - 1, jnp.int32)])
    rotation = jax.random.randint(key_turn, (), 0, SECTIONS)
    owners = jnp.roll(owners, rotation)
    section_keys = jax.random.split(key_local, SECTIONS)
    within = jnp.stack([jax.random.permutation(section_keys[section], IBH)[:PB] for section in range(SECTIONS)]).astype(jnp.int32)
    present = jnp.any(within == IBH - 1, axis=1)
    leading = jnp.where((owners == N_COL - 1) & jnp.logical_not(present), IBH - 1, within[:, 0])
    within = within.at[:, 0].set(leading.astype(jnp.int32))
    return (owners[:, None] * IBH + within).astype(jnp.int32)


def plant(values, stream_key, least, largest):
    longest = values.shape.index(max(values.shape))
    spots = []
    for shift in (0, 1):
        where = [jax.random.randint(jax.random.fold_in(stream_key, axis), (), 0, length) for axis, length in enumerate(values.shape)]
        where[longest] = (where[longest] + shift) % values.shape[longest]
        spots.append(tuple(where))
    return values.at[spots[0]].set(least).at[spots[1]].set(largest)


def steps_of(stream_key, dims, cuts, least, largest):
    factor_of = 1.0
    for position, blocks in cuts:
        heights = jax.random.uniform(jax.random.fold_in(jax.random.fold_in(stream_key, 6), position), (blocks,), jnp.float32, least / len(cuts), largest / len(cuts))
        factor_of = factor_of * jnp.repeat(jnp.exp(heights), dims[position] // blocks).reshape((-1,) + (1,) * (len(dims) - 1 - position))
    return factor_of


def centred(key, dims, spread, most, pieces=(), kind=jnp.bfloat16):
    values = jax.random.normal(key, dims, jnp.float32) * spread
    if len(pieces) > 0:
        values = steps_of(key, dims, pieces, -0.22, 0.18) * values
    return jnp.clip(values, min=-most, max=most).astype(kind)


def setup_inputs(seed: int = 0) -> dict:
    seeds = jax.random.split(jax.random.key(seed), 8)
    return {
        "hamiltonian": centred(seeds[0], (NA * BS, IN * BS), (SECTIONS * PB * BS) ** -0.5, 0.125, ((0, 16), (1, 32))),
        "z_panel": centred(seeds[1], (IN * BS, NJ * BS), 1.0, 6.0, ((0, 16), (1, 32))),
        "z_slab": centred(seeds[2], (NA * BS, NJ * BS), (NA * BS) ** -0.5, 0.125, ((0, 16), (1, 32))),
        "mask_h": plant((jax.random.randint(seeds[3], (NA, IN), 0, 3) < 1).astype(jnp.int32), jax.random.fold_in(seeds[3], 1), 0, 1),
        "mask_panel": plant((jax.random.randint(seeds[4], (IN, NJ), 0, 3) < 1).astype(jnp.int32), jax.random.fold_in(seeds[4], 1), 0, 1),
        "mask_slab": plant((jax.random.randint(seeds[5], (NA, NJ), 0, 3) < 1).astype(jnp.int32), jax.random.fold_in(seeds[5], 1), 0, 1),
        "section_blocks": draw_section_blocks(jax.random.fold_in(seeds[7], 71), 0),
    }


def expand_mask(values, mask):
    row_blocks, col_blocks = mask.shape
    grown = values.reshape(row_blocks, BS, col_blocks, BS) * mask.astype(values.dtype)[:, None, :, None]
    return grown.reshape(row_blocks * BS, col_blocks * BS)


def reference(hamiltonian, z_panel, z_slab, mask_h, mask_panel, mask_slab, section_blocks):
    slab_masked = expand_mask(z_slab, mask_slab)
    offsets = jnp.arange(BS, dtype=jnp.int32)
    summed = jnp.zeros((NA * BS, NJ * BS), jnp.float32)
    for section in range(SECTIONS):
        blocks = section_blocks[section].astype(jnp.int32)
        columns = (blocks[:, None] * BS + offsets[None, :]).reshape(-1).astype(jnp.int32)
        h_part = expand_mask(jnp.take(hamiltonian, columns, axis=1), jnp.take(mask_h, blocks, axis=1))
        z_part = expand_mask(jnp.take(z_panel, columns, axis=0), jnp.take(mask_panel, blocks, axis=0))
        summed = summed + jnp.dot(h_part, z_part, preferred_element_type=jnp.float32)
    product = summed.astype(jnp.bfloat16)
    grouped_y = product.reshape(N_ROW, RB * BS, NJ * BS)
    grouped_z = slab_masked.reshape(N_ROW, RB * BS, NJ * BS)

    def accumulate(carried, operands):
        group_term = lax.dot_general(operands[0], operands[1], (((0,), (0,)), ((), ())), preferred_element_type=jnp.float32)
        rounded = lax.optimization_barrier(group_term.astype(jnp.bfloat16))
        return carried + rounded.astype(jnp.float32), None

    initial = jnp.zeros((NJ * BS, NJ * BS), jnp.float32)
    total, unused = lax.scan(accumulate, initial, (grouped_y, grouped_z))
    return total.astype(jnp.bfloat16)
```

```python
import jax
import jax.numpy as jnp
from jax import lax
from jax.experimental import pallas as pl
from jax.experimental.pallas import tpu as pltpu
from jax.sharding import Mesh, PartitionSpec as P

BS = 64
LANES = 128
SECTIONS = 2
PICKS = 16
H_BLOCKS = 32
Z_BLOCKS = 64
ROW = ("zl", "y")
COL = ("x", "zh", "co")
PLANE = ("y", "x")
ALL = ROW + COL
SIZES = (4, 4, 4, 4, 2)

SMEM = pl.BlockSpec(memory_space=pltpu.SMEM)
VMEM = pl.BlockSpec(memory_space=pltpu.VMEM)


def owner_col(blocks, section):
    return blocks[section, 0] // H_BLOCKS


def owner_row(blocks, section):
    return blocks[section, 0] // Z_BLOCKS


def lane_mask(left, right):
    lane = lax.broadcasted_iota(jnp.int32, (1, LANES), 1)
    return jnp.where(lane < BS, left, right).astype(jnp.float32).astype(jnp.bfloat16)


def rows(index, size):
    return pl.ds(pl.multiple_of(index * size, size), size)


def pick_h_kernel(blocks, mask_h, h, picked, turned):
    me = (lax.axis_index("x") * 4 + lax.axis_index("zh")) * 2 + lax.axis_index("co")
    own = jnp.where(owner_col(blocks, 1) == me, 1, 0)
    for tile in range(h.shape[1] // LANES):
        at = slice(tile * LANES, (tile + 1) * LANES)
        turned[at, :] = h[:, at].T
    for p in range(PICKS):
        b = lax.rem(blocks[own, p], H_BLOCKS)
        picked[p] = turned[rows(b, BS), :] * lane_mask(mask_h[0, b], mask_h[1, b])


def pick_z_kernel(blocks, mask_panel, pair_h, z, packed):
    co = lax.axis_index("co")
    core = lax.rem(owner_col(blocks, co), 2)
    for p in range(PICKS):
        packed[p, 0] = pair_h[core, p]
        for s in range(SECTIONS):
            b = lax.rem(blocks[s, p], Z_BLOCKS)
            packed[p, 1 + s] = z[rows(b, BS), :] * lane_mask(mask_panel[b, 0], mask_panel[b, 1])


def choose_kernel(blocks, got, part_h, part_z):
    x0 = owner_col(blocks, lax.axis_index("co")) // 8
    for y in range(4):
        part_h[y] = got[4 * y + x0, 0]
    for s in range(SECTIONS):
        y0 = lax.rem(owner_row(blocks, s), 4)
        for x in range(4):
            part_z[s, x] = got[4 * y0 + x, 1 + s]


def product_kernel(blocks, all_h, all_z, out):
    z0 = [owner_row(blocks, s) // 4 for s in range(SECTIONS)]
    right = [
        jnp.concatenate([all_z[z0[s], s, x] for s in range(SECTIONS)], axis=0) for x in range(4)
    ]
    for y in range(4):
        left = jnp.concatenate([all_h[s, y] for s in range(SECTIONS)], axis=0)
        for x in range(4):
            out[4 * y + x] = lax.dot_general(
                left, right[x], (((0,), (0,)), ((), ())), preferred_element_type=jnp.float32
            ).astype(out.dtype)


def total_kernel(parts, copies):
    total = parts[0].astype(jnp.float32)
    for i in range(1, parts.shape[0]):
        total = total + parts[i].astype(jnp.float32)
    total = total.astype(copies.dtype)
    for i in range(copies.shape[0]):
        copies[i] = total


def last_kernel(y_col, slabs, out):
    for half in range(2):
        total = jnp.zeros((LANES, LANES), jnp.float32)
        for r in range(16):
            total = total + lax.dot_general(
                y_col[r],
                slabs[2 * r + half],
                (((0,), (0,)), ((), ())),
                preferred_element_type=jnp.float32,
            )
        out[half] = total.astype(out.dtype)


def shape(*dims):
    return jax.ShapeDtypeStruct(dims, jnp.bfloat16)


def expand_mask(values, mask):
    row_blocks, col_blocks = mask.shape
    grown = (
        values.reshape(row_blocks, BS, col_blocks, BS) * mask.astype(values.dtype)[:, None, :, None]
    )
    return grown.reshape(row_blocks * BS, col_blocks * BS)


def swapped_pairs():
    return [
        ((r * 16 + k) * 2 + co, (k * 16 + r) * 2 + co)
        for r in range(16)
        for k in range(16)
        for co in range(2)
    ]


def per_device(hamiltonian, z_panel, z_slab, mask_h, mask_panel, mask_slab, blocks):
    slab = expand_mask(z_slab, mask_slab)
    slab = lax.ppermute(slab, ALL, swapped_pairs())

    own_h = pl.pallas_call(
        pick_h_kernel,
        out_shape=shape(PICKS, BS, LANES),
        in_specs=[SMEM, SMEM, VMEM],
        out_specs=VMEM,
        scratch_shapes=[pltpu.VMEM((hamiltonian.shape[1], LANES), jnp.bfloat16)],
        name="pick_h",
    )(blocks, mask_h, hamiltonian)
    pair_h = lax.all_gather(own_h, "co", axis=0)
    slab, pair_h = lax.optimization_barrier((slab, pair_h))
    slabs = lax.all_gather(slab, COL, axis=0)
    packed = pl.pallas_call(
        pick_z_kernel,
        out_shape=shape(PICKS, 1 + SECTIONS, BS, LANES),
        in_specs=[SMEM, SMEM, VMEM, VMEM],
        out_specs=VMEM,
        name="pick_z",
    )(blocks, mask_panel, pair_h, z_panel)
    got = lax.all_to_all(packed, PLANE, 0, 0, tiled=True)
    part_h, part_z = pl.pallas_call(
        choose_kernel,
        out_shape=(shape(4, BS, LANES), shape(SECTIONS, 4, BS, LANES)),
        in_specs=[SMEM, VMEM],
        out_specs=(VMEM, VMEM),
        name="choose",
    )(blocks, got)
    all_z = lax.all_gather(part_z, "zl", axis=0)
    across = lax.all_gather(part_h, "zh", axis=0)
    zh0 = lax.rem(owner_col(blocks, lax.axis_index("co")) // 2, 4)
    all_h = lax.all_gather(
        lax.dynamic_index_in_dim(across, zh0, 0, keepdims=False), "co", axis=0
    )
    partial = pl.pallas_call(
        product_kernel,
        out_shape=shape(16, LANES, LANES),
        in_specs=[SMEM, VMEM, VMEM],
        out_specs=VMEM,
        name="product",
    )(blocks, all_h, all_z)
    partial = lax.all_to_all(partial, PLANE, 0, 0, tiled=True)
    slabs, partial = lax.optimization_barrier((slabs, partial))
    copies = pl.pallas_call(
        total_kernel,
        out_shape=shape(16, LANES, LANES),
        in_specs=[VMEM],
        out_specs=VMEM,
        name="total",
    )(partial)
    y_col = lax.all_to_all(copies, ROW, 0, 0, tiled=True)
    halves = pl.pallas_call(
        last_kernel,
        out_shape=shape(2, LANES, LANES),
        in_specs=[VMEM, VMEM],
        out_specs=VMEM,
        name="last",
    )(y_col, slabs)
    k_block = lax.all_to_all(halves, "co", 0, 0, tiled=True)
    return lax.ppermute(k_block.reshape(-1, LANES), ALL, swapped_pairs())


def solution(mesh):
    fine = Mesh(mesh.devices.reshape(SIZES), ALL)
    placed = (P(ROW, COL),) * 6 + (P(),)
    return jax.shard_map(
        per_device, mesh=fine, in_specs=placed, out_specs=P(ROW, COL), check_vma=False
    )
```

```python
import jax
import jax.numpy as jnp
from jax import lax
from jax.experimental import pallas as pl
from jax.experimental.pallas import tpu as pltpu
from jax.sharding import Mesh, PartitionSpec as P

BS = 64
LANES = 128
SECTIONS = 2
PICKS = 16
H_BLOCKS = 32
Z_BLOCKS = 64
ROW = ("zl", "y")
COL = ("x", "zh", "co")
PLANE = ("y", "x")
ALL = ROW + COL
SIZES = (4, 4, 4, 4, 2)

SMEM = pl.BlockSpec(memory_space=pltpu.SMEM)
VMEM = pl.BlockSpec(memory_space=pltpu.VMEM)


def owner_col(blocks, section):
    return blocks[section, 0] // H_BLOCKS


def owner_row(blocks, section):
    return blocks[section, 0] // Z_BLOCKS


def lane_mask(left, right):
    lane = lax.broadcasted_iota(jnp.int32, (1, LANES), 1)
    return jnp.where(lane < BS, left, right).astype(jnp.float32).astype(jnp.bfloat16)


def rows(index, size):
    return pl.ds(pl.multiple_of(index * size, size), size)


def pick_kernel(blocks, mask_h, mask_panel, mask_slab, h, z, slab, packed, masked, turned):
    me = (lax.axis_index("x") * 4 + lax.axis_index("zh")) * 2 + lax.axis_index("co")
    own = jnp.where(owner_col(blocks, 1) == me, 1, 0)
    for tile in range(h.shape[1] // LANES):
        at = slice(tile * LANES, (tile + 1) * LANES)
        turned[at, :] = h[:, at].T
    for p in range(PICKS):
        b = lax.rem(blocks[own, p], H_BLOCKS)
        packed[p, 0] = turned[rows(b, BS), :] * lane_mask(mask_h[0, b], mask_h[1, b])
        for s in range(SECTIONS):
            b = lax.rem(blocks[s, p], Z_BLOCKS)
            packed[p, 1 + s] = z[rows(b, BS), :] * lane_mask(mask_panel[0, b], mask_panel[1, b])
    for i in range(2):
        at = slice(i * BS, (i + 1) * BS)
        masked[i] = slab[at, :] * lane_mask(mask_slab[i, 0], mask_slab[i, 1])


def choose_kernel(blocks, got, part_h, part_z):
    for s in range(SECTIONS):
        x0 = owner_col(blocks, s) // 8
        y0 = lax.rem(owner_row(blocks, s), 4)
        for i in range(4):
            part_h[s, i] = got[4 * i + x0, 0]
            block = got[4 * y0 + i, 1 + s]
            for copy in range(4):
                part_z[copy, s, i] = block


def product_kernel(blocks, pair, all_z, out):
    z0 = [owner_row(blocks, s) // 4 for s in range(SECTIONS)]
    right = [
        jnp.concatenate([all_z[z0[s], s, x] for s in range(SECTIONS)], axis=0) for x in range(4)
    ]
    for y in range(4):
        left = jnp.concatenate([pair[s, y] for s in range(SECTIONS)], axis=0)
        for x in range(4):
            out[4 * y + x] = lax.dot_general(
                left, right[x], (((0,), (0,)), ((), ())), preferred_element_type=jnp.float32
            ).astype(out.dtype)


def total_kernel(parts, copies):
    total = parts[0].astype(jnp.float32)
    for i in range(1, parts.shape[0]):
        total = total + parts[i].astype(jnp.float32)
    total = total.astype(copies.dtype)
    for i in range(copies.shape[0]):
        copies[i] = total


def last_kernel(y_col, *slabs_and_out):
    slabs, out = slabs_and_out[:-1], slabs_and_out[-1]
    for core in range(2):
        total = jnp.zeros((LANES, LANES), jnp.float32)
        for back, slab in zip((0, 1, 3, 2), slabs):
            x = lax.rem(lax.axis_index("x") + 4 - back, 4)
            for zh in range(4):
                right = jnp.concatenate([slab[core, 2 * zh + i] for i in range(2)], axis=0)
                total = total + lax.dot_general(
                    y_col[4 * x + zh],
                    right,
                    (((0,), (0,)), ((), ())),
                    preferred_element_type=jnp.float32,
                )
        out[core] = total.astype(out.dtype)


def shape(*dims):
    return jax.ShapeDtypeStruct(dims, jnp.bfloat16)


def swapped_pairs():
    return [
        ((r * 16 + k) * 2 + co, (k * 16 + r) * 2 + co)
        for r in range(16)
        for k in range(16)
        for co in range(2)
    ]


def per_device(hamiltonian, z_panel, z_slab, mask_h, mask_panel, mask_slab, blocks):
    packed, slab = pl.pallas_call(
        pick_kernel,
        out_shape=(shape(PICKS, 1 + SECTIONS, BS, LANES), shape(2, BS, LANES)),
        in_specs=[SMEM] * 4 + [VMEM] * 3,
        out_specs=(VMEM, VMEM),
        scratch_shapes=[pltpu.VMEM((hamiltonian.shape[1], LANES), jnp.bfloat16)],
        name="pick",
    )(blocks, mask_h, mask_panel.T, mask_slab, hamiltonian, z_panel, z_slab)
    slab = lax.ppermute(slab, ALL, swapped_pairs())
    got = lax.all_to_all(packed, PLANE, 0, 0, tiled=True)
    slab, got = lax.optimization_barrier((slab, got))
    part_h, part_z = pl.pallas_call(
        choose_kernel,
        out_shape=(shape(SECTIONS, 4, BS, LANES), shape(4, SECTIONS, 4, BS, LANES)),
        in_specs=[SMEM, VMEM],
        out_specs=(VMEM, VMEM),
        name="choose",
    )(blocks, got)
    all_z = lax.all_to_all(part_z, "zl", 0, 0, tiled=True)
    core = lax.axis_index("co")
    first = jnp.where(core == 0, blocks[0, 0], blocks[1, 0])
    owner_core = lax.shift_right_logical(first, 5) & 1
    owner_zh = lax.shift_right_logical(first, 6) & 3
    pair_h = lax.all_gather(part_h, "co", axis=0)
    mine_h = lax.dynamic_slice(
        pair_h, (owner_core, core, 0, 0, 0), (1, 1) + part_h.shape[1:]
    )
    across = lax.all_gather(jnp.concatenate([mine_h[0, 0], slab], axis=0), "zh", axis=0)
    from_owner = lax.dynamic_index_in_dim(across[:, :4], owner_zh, 0, keepdims=False)
    pair = lax.all_gather(
        jnp.concatenate([from_owner, across[:, 4:].reshape(8, BS, LANES)], axis=0), "co", axis=0
    )
    partial = pl.pallas_call(
        product_kernel,
        out_shape=shape(16, LANES, LANES),
        in_specs=[SMEM, VMEM, VMEM],
        out_specs=VMEM,
        name="product",
    )(blocks, pair, all_z)
    partial = lax.all_to_all(partial, PLANE, 0, 0, tiled=True)
    slabs = [pair[:, 4:]]
    for back in (1, 3, 2):
        slabs.append(lax.ppermute(slabs[0], "x", [(x, (x + back) % 4) for x in range(4)]))
    slabs[1], slabs[2], partial = lax.optimization_barrier((slabs[1], slabs[2], partial))
    copies = pl.pallas_call(
        total_kernel,
        out_shape=shape(16, LANES, LANES),
        in_specs=[VMEM],
        out_specs=VMEM,
        name="total",
    )(partial)
    y_col = lax.all_to_all(copies, ROW, 0, 0, tiled=True)
    halves = pl.pallas_call(
        last_kernel,
        out_shape=shape(2, LANES, LANES),
        in_specs=[VMEM] * 5,
        out_specs=VMEM,
        name="last",
    )(y_col, *slabs)
    k_block = lax.all_to_all(halves, "co", 0, 0, tiled=True)
    return lax.ppermute(k_block.reshape(-1, LANES), ALL, swapped_pairs())


def solution(mesh):
    fine = Mesh(mesh.devices.reshape(SIZES), ALL)
    placed = (P(ROW, COL),) * 6 + (P(),)
    return jax.shard_map(
        per_device, mesh=fine, in_specs=placed, out_specs=P(ROW, COL), check_vma=False
    )
```

```python
import jax
import jax.numpy as jnp
from jax import lax
from jax.experimental import pallas as pl
from jax.experimental.pallas import tpu as pltpu
from jax.sharding import Mesh, PartitionSpec as P

BS = 64
LANES = 128
SECTIONS = 2
PICKS = 16
H_BLOCKS = 32
Z_BLOCKS = 64
ROW = ("zl", "y")
COL = ("x", "zh", "co")
PLANE = ("y", "x")
ALL = ROW + COL
SIZES = (4, 4, 4, 4, 2)

SMEM = pl.BlockSpec(memory_space=pltpu.SMEM)
VMEM = pl.BlockSpec(memory_space=pltpu.VMEM)


def owner_col(blocks, section):
    return blocks[section, 0] // H_BLOCKS


def owner_row(blocks, section):
    return blocks[section, 0] // Z_BLOCKS


def lane_mask(left, right):
    lane = lax.broadcasted_iota(jnp.int32, (1, LANES), 1)
    return jnp.where(lane < BS, left, right).astype(jnp.float32).astype(jnp.bfloat16)


def rows(index, size):
    return pl.ds(pl.multiple_of(index * size, size), size)


def pick_kernel(blocks, mask_h, mask_panel, mask_slab, h, z, slab, packed, masked, turned):
    me = (lax.axis_index("x") * 4 + lax.axis_index("zh")) * 2 + lax.axis_index("co")
    own = jnp.where(owner_col(blocks, 1) == me, 1, 0)
    for tile in range(h.shape[1] // LANES):
        at = slice(tile * LANES, (tile + 1) * LANES)
        turned[at, :] = h[:, at].T
    for p in range(PICKS):
        b = lax.rem(blocks[own, p], H_BLOCKS)
        packed[p, 0] = turned[rows(b, BS), :] * lane_mask(mask_h[0, b], mask_h[1, b])
        for s in range(SECTIONS):
            b = lax.rem(blocks[s, p], Z_BLOCKS)
            packed[p, 1 + s] = z[rows(b, BS), :] * lane_mask(mask_panel[0, b], mask_panel[1, b])
    for i in range(2):
        at = slice(i * BS, (i + 1) * BS)
        masked[i] = slab[at, :] * lane_mask(mask_slab[i, 0], mask_slab[i, 1])


def choose_kernel(blocks, got, part_h, part_z):
    place = lax.axis_index("zh") * 2 + lax.axis_index("co")
    for s in range(SECTIONS):
        x0 = owner_col(blocks, s) // 8
        y0 = lax.rem(owner_row(blocks, s), 4)
        owned = jnp.where(lax.rem(owner_col(blocks, s), 8) == place, 1, 0)
        for i in range(4):
            part_h[s, i] = got[4 * i + x0, 0] * lane_mask(owned, owned)
            block = got[4 * y0 + i, 1 + s]
            for copy in range(4):
                part_z[copy, s, i] = block


def product_kernel(blocks, pair, all_z, out):
    z0 = [owner_row(blocks, s) // 4 for s in range(SECTIONS)]
    zh0 = [lax.rem(owner_col(blocks, s) // 2, 4) for s in range(SECTIONS)]
    right = [
        jnp.concatenate([all_z[z0[s], s, x] for s in range(SECTIONS)], axis=0) for x in range(4)
    ]
    for y in range(4):
        left = jnp.concatenate([pair[s, zh0[s], y] for s in range(SECTIONS)], axis=0)
        for x in range(4):
            out[4 * y + x] = lax.dot_general(
                left, right[x], (((0,), (0,)), ((), ())), preferred_element_type=jnp.float32
            ).astype(out.dtype)


def total_kernel(parts, copies):
    total = parts[0].astype(jnp.float32)
    for i in range(1, parts.shape[0]):
        total = total + parts[i].astype(jnp.float32)
    total = total.astype(copies.dtype)
    for i in range(copies.shape[0]):
        copies[i] = total


def last_kernel(y_col, own, two, one, three, swapped, out):
    co = lax.axis_index("co")
    here = (own.at[co], two.at[co], one, three)
    there = (own.at[1 - co], two.at[1 - co], swapped.at[0], swapped.at[1])
    for core, slabs in ((co, here), (1 - co, there)):
        total = jnp.zeros((LANES, LANES), jnp.float32)
        for back, slab in zip((0, 2, 1, 3), slabs):
            x = lax.rem(lax.axis_index("x") + 4 - back, 4)
            for zh in range(4):
                total = total + lax.dot_general(
                    y_col[4 * x + zh],
                    slab[zh],
                    (((0,), (0,)), ((), ())),
                    preferred_element_type=jnp.float32,
                )
        out[core] = total.astype(out.dtype)


def shape(*dims):
    return jax.ShapeDtypeStruct(dims, jnp.bfloat16)


def swapped_pairs():
    return [
        ((r * 16 + k) * 2 + co, (k * 16 + r) * 2 + co)
        for r in range(16)
        for k in range(16)
        for co in range(2)
    ]


def per_device(hamiltonian, z_panel, z_slab, mask_h, mask_panel, mask_slab, blocks):
    packed, slab = pl.pallas_call(
        pick_kernel,
        out_shape=(shape(PICKS, 1 + SECTIONS, BS, LANES), shape(2, BS, LANES)),
        in_specs=[SMEM] * 4 + [VMEM] * 3,
        out_specs=(VMEM, VMEM),
        scratch_shapes=[pltpu.VMEM((hamiltonian.shape[1], LANES), jnp.bfloat16)],
        name="pick",
    )(blocks, mask_h, mask_panel.T, mask_slab, hamiltonian, z_panel, z_slab)
    slab = lax.ppermute(slab, ALL, swapped_pairs())
    got = lax.all_to_all(packed, PLANE, 0, 0, tiled=True)
    slab, got = lax.optimization_barrier((slab, got))
    part_h, part_z = pl.pallas_call(
        choose_kernel,
        out_shape=(shape(SECTIONS, 4, BS, LANES), shape(4, SECTIONS, 4, BS, LANES)),
        in_specs=[SMEM, VMEM],
        out_specs=(VMEM, VMEM),
        name="choose",
    )(blocks, got)
    all_z = lax.all_to_all(part_z, "zl", 0, 0, tiled=True)
    core = lax.axis_index("co")
    pair_h = lax.all_gather(part_h, "co", axis=0)
    mine_h = lax.dynamic_index_in_dim(pair_h, core, 1, keepdims=False)
    mine_h = mine_h[0] + mine_h[1]
    across = lax.all_gather(jnp.concatenate([mine_h, slab], axis=0), "zh", axis=0)
    pair = lax.all_gather(across, "co", axis=0)
    partial = pl.pallas_call(
        product_kernel,
        out_shape=shape(16, LANES, LANES),
        in_specs=[SMEM, VMEM, VMEM],
        out_specs=VMEM,
        name="product",
    )(blocks, pair, all_z)
    partial = lax.all_to_all(partial, PLANE, 0, 0, tiled=True)
    own = across[:, 4:].reshape(4, LANES, LANES)
    both = pair[:, :, 4:].reshape(2, 4, LANES, LANES)
    one, three = [
        lax.ppermute(own, "x", [(x, (x + back) % 4) for x in range(4)]) for back in (1, 3)
    ]
    two = lax.ppermute(both, "x", [(x, (x + 2) % 4) for x in range(4)])
    one, three, partial = lax.optimization_barrier((one, three, partial))
    swapped = lax.ppermute(jnp.stack([one, three]), "co", [(0, 1), (1, 0)])
    copies = pl.pallas_call(
        total_kernel,
        out_shape=shape(16, LANES, LANES),
        in_specs=[VMEM],
        out_specs=VMEM,
        name="total",
    )(partial)
    y_col = lax.all_to_all(copies, ROW, 0, 0, tiled=True)
    halves = pl.pallas_call(
        last_kernel,
        out_shape=shape(2, LANES, LANES),
        in_specs=[VMEM] * 6,
        out_specs=VMEM,
        name="last",
    )(y_col, both, two, one, three, swapped)
    k_block = lax.all_to_all(halves, "co", 0, 0, tiled=True)
    return lax.ppermute(k_block.reshape(-1, LANES), ALL, swapped_pairs())


def solution(mesh):
    fine = Mesh(mesh.devices.reshape(SIZES), ALL)
    placed = (P(ROW, COL),) * 6 + (P(),)
    return jax.shard_map(
        per_device, mesh=fine, in_specs=placed, out_specs=P(ROW, COL), check_vma=False
    )
```

```python
import jax
import jax.numpy as jnp
from jax import lax
from jax.experimental import pallas as pl
from jax.experimental.pallas import tpu as pltpu
from jax.sharding import Mesh, PartitionSpec as P

BS = 64
LANES = 128
SECTIONS = 2
PICKS = 16
H_BLOCKS = 32
Z_BLOCKS = 64
ROW = ("zl", "y")
COL = ("x", "zh", "co")
PLANE = ("y", "x")
ALL = ROW + COL
SIZES = (4, 4, 4, 4, 2)

SMEM = pl.BlockSpec(memory_space=pltpu.SMEM)
VMEM = pl.BlockSpec(memory_space=pltpu.VMEM)


def owner_col(blocks, section):
    return blocks[section, 0] // H_BLOCKS


def owner_row(blocks, section):
    return blocks[section, 0] // Z_BLOCKS


def lane_mask(left, right):
    lane = lax.broadcasted_iota(jnp.int32, (1, LANES), 1)
    return jnp.where(lane < BS, left, right).astype(jnp.float32).astype(jnp.bfloat16)


def rows(index, size):
    return pl.ds(pl.multiple_of(index * size, size), size)


def pick_kernel(blocks, mask_h, mask_panel, mask_slab, h, z, slab, packed, masked, turned):
    me = (lax.axis_index("x") * 4 + lax.axis_index("zh")) * 2 + lax.axis_index("co")
    own = jnp.where(owner_col(blocks, 1) == me, 1, 0)
    for tile in range(h.shape[1] // LANES):
        at = slice(tile * LANES, (tile + 1) * LANES)
        turned[at, :] = h[:, at].T
    for p in range(PICKS):
        b = lax.rem(blocks[own, p], H_BLOCKS)
        packed[p, 0] = turned[rows(b, BS), :] * lane_mask(mask_h[0, b], mask_h[1, b])
        for s in range(SECTIONS):
            b = lax.rem(blocks[s, p], Z_BLOCKS)
            packed[p, 1 + s] = z[rows(b, BS), :] * lane_mask(mask_panel[0, b], mask_panel[1, b])
    for i in range(2):
        at = slice(i * BS, (i + 1) * BS)
        masked[i] = slab[at, :] * lane_mask(mask_slab[i, 0], mask_slab[i, 1])


def product_kernel(blocks, pair, all_z, out):
    z0 = [owner_row(blocks, s) // 4 for s in range(SECTIONS)]
    zh0 = [lax.rem(owner_col(blocks, s) // 2, 4) for s in range(SECTIONS)]
    right = [
        jnp.concatenate([all_z[z0[s], s, x] for s in range(SECTIONS)], axis=0) for x in range(4)
    ]
    for y in range(4):
        left = jnp.concatenate([pair[s, zh0[s], y] for s in range(SECTIONS)], axis=0)
        for x in range(4):
            out[4 * y + x] = lax.dot_general(
                left, right[x], (((0,), (0,)), ((), ())), preferred_element_type=jnp.float32
            ).astype(out.dtype)


def last_kernel(y_col, own, two, one, three, swapped, out):
    co = lax.axis_index("co")
    here = (own.at[co], two.at[co], one, three)
    there = (own.at[1 - co], two.at[1 - co], swapped.at[0], swapped.at[1])
    for core, slabs in ((co, here), (1 - co, there)):
        total = jnp.zeros((LANES, LANES), jnp.float32)
        for back, slab in zip((0, 2, 1, 3), slabs):
            x = lax.rem(lax.axis_index("x") + 4 - back, 4)
            for zh in range(4):
                total = total + lax.dot_general(
                    y_col[4 * x + zh],
                    slab[zh],
                    (((0,), (0,)), ((), ())),
                    preferred_element_type=jnp.float32,
                )
        out[core] = total.astype(out.dtype)


def shape(*dims):
    return jax.ShapeDtypeStruct(dims, jnp.bfloat16)


def swapped_pairs():
    return [
        ((r * 16 + k) * 2 + co, (k * 16 + r) * 2 + co)
        for r in range(16)
        for k in range(16)
        for co in range(2)
    ]


def per_device(hamiltonian, z_panel, z_slab, mask_h, mask_panel, mask_slab, blocks):
    packed, slab = pl.pallas_call(
        pick_kernel,
        out_shape=(shape(PICKS, 1 + SECTIONS, BS, LANES), shape(2, BS, LANES)),
        in_specs=[SMEM] * 4 + [VMEM] * 3,
        out_specs=(VMEM, VMEM),
        scratch_shapes=[pltpu.VMEM((hamiltonian.shape[1], LANES), jnp.bfloat16)],
        name="pick",
    )(blocks, mask_h, mask_panel.T, mask_slab, hamiltonian, z_panel, z_slab)
    slab = lax.ppermute(slab, ALL, swapped_pairs())
    got = lax.all_to_all(packed, PLANE, 0, 0, tiled=True)
    first = [blocks[s, 0] for s in range(SECTIONS)]
    place = lax.axis_index("zh") * 2 + lax.axis_index("co")
    outer = [lax.shift_right_logical(f, 8) for f in first]
    inner = [lax.shift_right_logical(f, 6) & 3 for f in first]
    owned = [
        ((lax.shift_right_logical(f, 5) & 7) == place).astype(jnp.bfloat16) for f in first
    ]
    outer, inner, owned, got = lax.optimization_barrier((outer, inner, owned, got))
    got = got.reshape(4, 4, 1 + SECTIONS, BS, LANES)
    part_h = jnp.stack(
        [
            lax.dynamic_index_in_dim(got[:, :, 0], outer[s], 1, keepdims=False) * owned[s]
            for s in range(SECTIONS)
        ]
    )
    part_z = jnp.stack(
        [
            lax.dynamic_index_in_dim(got[:, :, 1 + s], inner[s], 0, keepdims=False)
            for s in range(SECTIONS)
        ]
    )
    part_z = jnp.broadcast_to(part_z, (4,) + part_z.shape)
    slab, part_h, part_z = lax.optimization_barrier((slab, part_h, part_z))
    all_z = lax.all_to_all(part_z, "zl", 0, 0, tiled=True)
    core = lax.axis_index("co")
    pair_h = lax.all_gather(part_h, "co", axis=0)
    mine_h = lax.dynamic_index_in_dim(pair_h, core, 1, keepdims=False)
    mine_h = mine_h[0] + mine_h[1]
    across = lax.all_gather(jnp.concatenate([mine_h, slab], axis=0), "zh", axis=0)
    pair = lax.all_gather(across, "co", axis=0)
    partial = pl.pallas_call(
        product_kernel,
        out_shape=shape(16, LANES, LANES),
        in_specs=[SMEM, VMEM, VMEM],
        out_specs=VMEM,
        name="product",
    )(blocks, pair, all_z)
    partial = lax.all_to_all(partial, PLANE, 0, 0, tiled=True)
    own = across[:, 4:].reshape(4, LANES, LANES)
    both = pair[:, :, 4:].reshape(2, 4, LANES, LANES)
    one, three = [
        lax.ppermute(own, "x", [(x, (x + back) % 4) for x in range(4)]) for back in (1, 3)
    ]
    two = lax.ppermute(both, "x", [(x, (x + 2) % 4) for x in range(4)])
    one, three, partial = lax.optimization_barrier((one, three, partial))
    swapped = lax.ppermute(jnp.stack([one, three]), "co", [(0, 1), (1, 0)])
    total = jnp.sum(partial.astype(jnp.float32), axis=0).astype(jnp.bfloat16)
    copies = jnp.broadcast_to(total, partial.shape)
    y_col = lax.all_to_all(copies, ROW, 0, 0, tiled=True)
    halves = pl.pallas_call(
        last_kernel,
        out_shape=shape(2, LANES, LANES),
        in_specs=[VMEM] * 6,
        out_specs=VMEM,
        name="last",
    )(y_col, both, two, one, three, swapped)
    k_block = lax.all_to_all(halves, "co", 0, 0, tiled=True)
    return lax.ppermute(k_block.reshape(-1, LANES), ALL, swapped_pairs())


def solution(mesh):
    fine = Mesh(mesh.devices.reshape(SIZES), ALL)
    placed = (P(ROW, COL),) * 6 + (P(),)
    return jax.shard_map(
        per_device, mesh=fine, in_specs=placed, out_specs=P(ROW, COL), check_vma=False
    )
```

```python
import functools

import jax
import jax.numpy as jnp
from jax import lax
from jax.experimental import pallas as pl
from jax.experimental.pallas import tpu as pltpu
from jax.sharding import Mesh, PartitionSpec as P

BS = 64
LANES = 128
SECTIONS = 2
PICKS = 16
H_BLOCKS = 32
Z_BLOCKS = 64
ROW = ("zl", "y")
COL = ("x", "zh", "co")
PLANE = ("y", "x")
ALL = ROW + COL
SIZES = (4, 4, 4, 4, 2)

SMEM = pl.BlockSpec(memory_space=pltpu.SMEM)
VMEM = pl.BlockSpec(memory_space=pltpu.VMEM)


def owner_col(blocks, section):
    return blocks[section, 0] // H_BLOCKS


def owner_row(blocks, section):
    return blocks[section, 0] // Z_BLOCKS


def lane_mask(left, right):
    lane = lax.broadcasted_iota(jnp.int32, (1, LANES), 1)
    return jnp.where(lane < BS, left, right).astype(jnp.float32).astype(jnp.bfloat16)


def rows(index, size):
    return pl.ds(pl.multiple_of(index * size, size), size)


def pick_kernel(blocks, mask_h, mask_panel, mask_slab, h, z, slab, packed, masked, turned):
    me = (lax.axis_index("x") * 4 + lax.axis_index("zh")) * 2 + lax.axis_index("co")
    own = jnp.where(owner_col(blocks, 1) == me, 1, 0)
    for tile in range(h.shape[1] // LANES):
        at = slice(tile * LANES, (tile + 1) * LANES)
        turned[at, :] = h[:, at].T
    for p in range(PICKS):
        b = lax.rem(blocks[own, p], H_BLOCKS)
        packed[p, 0] = turned[rows(b, BS), :] * lane_mask(mask_h[0, b], mask_h[1, b])
        for s in range(SECTIONS):
            b = lax.rem(blocks[s, p], Z_BLOCKS)
            packed[p, 1 + s] = z[rows(b, BS), :] * lane_mask(mask_panel[0, b], mask_panel[1, b])
    for i in range(2):
        at = slice(i * BS, (i + 1) * BS)
        masked[i] = slab[at, :] * lane_mask(mask_slab[i, 0], mask_slab[i, 1])


def product_kernel(single, blocks, pair, all_z, out):
    z0 = [owner_row(blocks, s) // 4 for s in range(SECTIONS)]
    zh0 = [lax.rem(owner_col(blocks, s) // 2, 4) for s in range(SECTIONS)]
    right = [
        jnp.concatenate([all_z[z0[s], 0 if single else s, x] for s in range(SECTIONS)], axis=0)
        for x in range(4)
    ]
    for y in range(4):
        left = jnp.concatenate([pair[s, zh0[s], y] for s in range(SECTIONS)], axis=0)
        for x in range(4):
            out[4 * y + x] = lax.dot_general(
                left, right[x], (((0,), (0,)), ((), ())), preferred_element_type=jnp.float32
            ).astype(out.dtype)


def last_kernel(y_col, own, two, one, three, swapped, out):
    co = lax.axis_index("co")
    here = (own.at[co], two.at[co], one, three)
    there = (own.at[1 - co], two.at[1 - co], swapped.at[0], swapped.at[1])
    for core, slabs in ((co, here), (1 - co, there)):
        total = jnp.zeros((LANES, LANES), jnp.float32)
        for back, slab in zip((0, 2, 1, 3), slabs):
            x = lax.rem(lax.axis_index("x") + 4 - back, 4)
            for zh in range(4):
                total = total + lax.dot_general(
                    y_col[4 * x + zh],
                    slab[zh],
                    (((0,), (0,)), ((), ())),
                    preferred_element_type=jnp.float32,
                )
        out[core] = total.astype(out.dtype)


def shape(*dims):
    return jax.ShapeDtypeStruct(dims, jnp.bfloat16)


def swapped_pairs():
    return [
        ((r * 16 + k) * 2 + co, (k * 16 + r) * 2 + co)
        for r in range(16)
        for k in range(16)
        for co in range(2)
    ]


def per_device(hamiltonian, z_panel, z_slab, mask_h, mask_panel, mask_slab, blocks):
    packed, slab = pl.pallas_call(
        pick_kernel,
        out_shape=(shape(PICKS, 1 + SECTIONS, BS, LANES), shape(2, BS, LANES)),
        in_specs=[SMEM] * 4 + [VMEM] * 3,
        out_specs=(VMEM, VMEM),
        scratch_shapes=[pltpu.VMEM((hamiltonian.shape[1], LANES), jnp.bfloat16)],
        name="pick",
    )(blocks, mask_h, mask_panel.T, mask_slab, hamiltonian, z_panel, z_slab)
    slab = lax.ppermute(slab, ALL, swapped_pairs())
    got = lax.all_to_all(packed, PLANE, 0, 0, tiled=True)
    first = [blocks[s, 0] for s in range(SECTIONS)]
    place = lax.axis_index("zh") * 2 + lax.axis_index("co")
    outer = [lax.shift_right_logical(f, 8) for f in first]
    inner = [lax.shift_right_logical(f, 6) & 3 for f in first]
    owned = [
        ((lax.shift_right_logical(f, 5) & 7) == place).astype(jnp.bfloat16) for f in first
    ]
    outer, inner, owned, got = lax.optimization_barrier((outer, inner, owned, got))
    got = got.reshape(4, 4, 1 + SECTIONS, BS, LANES)
    part_h = jnp.stack(
        [
            lax.dynamic_index_in_dim(got[:, :, 0], outer[s], 1, keepdims=False) * owned[s]
            for s in range(SECTIONS)
        ]
    )
    part_z = jnp.stack(
        [
            lax.dynamic_index_in_dim(got[:, :, 1 + s], inner[s], 0, keepdims=False)
            for s in range(SECTIONS)
        ]
    )
    slab, part_h, part_z = lax.optimization_barrier((slab, part_h, part_z))
    core = lax.axis_index("co")

    def partial_product(part_z, single):
        all_z = lax.all_to_all(
            jnp.broadcast_to(part_z, (4,) + part_z.shape), "zl", 0, 0, tiled=True
        )
        pair_h = lax.all_gather(part_h, "co", axis=0)
        mine_h = lax.dynamic_index_in_dim(pair_h, core, 1, keepdims=False)
        mine_h = mine_h[0] + mine_h[1]
        across = lax.all_gather(jnp.concatenate([mine_h, slab], axis=0), "zh", axis=0)
        pair = lax.all_gather(across, "co", axis=0)
        partial = pl.pallas_call(
            functools.partial(product_kernel, single),
            out_shape=shape(16, LANES, LANES),
            in_specs=[SMEM, VMEM, VMEM],
            out_specs=VMEM,
            name="product",
        )(blocks, pair, all_z)
        return partial, across, pair

    own_section = jnp.where(outer[1] == lax.axis_index("zl"), 1, 0)
    partial, across, pair = lax.cond(
        outer[0] == outer[1],
        lambda: partial_product(part_z, False),
        lambda: partial_product(lax.dynamic_slice_in_dim(part_z, own_section, 1, 0), True),
    )
    partial = lax.all_to_all(partial, PLANE, 0, 0, tiled=True)
    own = across[:, 4:].reshape(4, LANES, LANES)
    both = pair[:, :, 4:].reshape(2, 4, LANES, LANES)
    one, three = [
        lax.ppermute(own, "x", [(x, (x + back) % 4) for x in range(4)]) for back in (1, 3)
    ]
    two = lax.ppermute(both, "x", [(x, (x + 2) % 4) for x in range(4)])
    one, three, partial = lax.optimization_barrier((one, three, partial))
    swapped = lax.ppermute(jnp.stack([one, three]), "co", [(0, 1), (1, 0)])
    total = jnp.sum(partial.astype(jnp.float32), axis=0).astype(jnp.bfloat16)
    copies = jnp.broadcast_to(total, partial.shape)
    y_col = lax.all_to_all(copies, ROW, 0, 0, tiled=True)
    halves = pl.pallas_call(
        last_kernel,
        out_shape=shape(2, LANES, LANES),
        in_specs=[VMEM] * 6,
        out_specs=VMEM,
        name="last",
    )(y_col, both, two, one, three, swapped)
    k_block = lax.all_to_all(halves, "co", 0, 0, tiled=True)
    return lax.ppermute(k_block.reshape(-1, LANES), ALL, swapped_pairs())


def solution(mesh):
    fine = Mesh(mesh.devices.reshape(SIZES), ALL)
    placed = (P(ROW, COL),) * 6 + (P(),)
    return jax.shard_map(
        per_device, mesh=fine, in_specs=placed, out_specs=P(ROW, COL), check_vma=False
    )
```
